256 devices in a mesh: lon: 64 (over x_hi, y, z), lat: 4 (over x_lo, core).
Axes of the slice: x: 4 (x_hi: 2, x_lo: 2; x = x_hi * 2 + x_lo), y: 4, z: 8, core: 2. Of those that a mesh axis runs over, the one named last changes fastest.
Arguments:
- queries: bfloat16 [4, 64, 128, 1536], P(None, 'lat', 'lon'), may hold values from -100 to 100
- token_keys: bfloat16 [4, 64, 128, 1536], P(None, 'lat', 'lon'), may hold values from -6 to 6
- token_values: bfloat16 [4, 64, 128, 1536], P(None, 'lat', 'lon'), may hold values from -6 to 6
- memory_bank: bfloat16 [2, 8, 64, 128, 1536], P(None, None, 'lat', 'lon'), may hold values from -6 to 6
- memory_ids: int32 [4, 64, 8], P('lat', 'lon'), may hold values from 0 to 511, as said below
- memory_count: int32 [4, 64], P('lat', 'lon'), may hold values from 7 to 8
Outputs:
- attended: bfloat16 [4, 64, 128, 1536], P(None, 'lat', 'lon')
The draws below stay inside these ranges and needn't reach their ends.
Inputs may be any that keep to these rules, and one draw needn't show every extreme that they name: `memory_ids`: entry v of tile (a, b) names slot v mod 8 of the tile (a, v // 8) of the same band, whose longitude tile lies within 2 tiles of b around the closed loop. Within one list no block appears twice and at most 4 entries name one owner tile; the first 4 entries all name one owner tile.
All inputs are finite; a program needn't handle non-finite values.
Results may differ from the reference program's by a relative error of at most 0.003.
Values may be sent and summed in bfloat16 or wider, within the bound.
No kernel may reach another device: no remote copies, remote signals or barrier semaphores. Data moves between devices by JAX's collectives and lax.ppermute only.
A program may use at most 64 MiB of HBM per device.

```python
import jax
import jax.numpy as jnp
from jax import lax

HEADS = 12
HEAD_DIM = 128
FRAMES = 4
LAT_DEV = 16
LON_DEV = 2
MEM_DEV = 8
TOPM = 8
CAP = 4
REACH = 2
LAT = 64
LON = 128
N_LON = 64
N_LAT = 4


def draw_queries(key, part):
    key = jax.random.fold_in(key, 1)
    first_key = jax.random.fold_in(key, 0)
    shape = (FRAMES, LAT, LON, HEADS * HEAD_DIM)
    return jnp.clip(2.5 * jax.random.normal(first_key, shape, jnp.float32), -15.0, 15.0).astype(jnp.bfloat16)


def draw_token_keys(key, part):
    key = jax.random.fold_in(key, 2)
    shape = (FRAMES, LAT, LON, HEADS * HEAD_DIM)
    return jnp.clip(jax.random.normal(key, shape, jnp.float32), -6.0, 6.0).astype(jnp.bfloat16)


def draw_memory_bank(key, part):
    key = jax.random.fold_in(key, 3)
    shape = (2, MEM_DEV, LAT, LON, HEADS * HEAD_DIM)
    return jnp.clip(jax.random.normal(key, shape, jnp.float32), -6.0, 6.0).astype(jnp.bfloat16)


def draw_memory_ids(key, part):
    key = jax.random.fold_in(key, 5)
    busy_key, rest_key, perm_key = jax.random.split(key, 3)
    tile_total = N_LAT * N_LON
    span_count = 2 * REACH + 1
    busy = jax.random.randint(busy_key, (tile_total,), 0, span_count)
    others = jax.random.randint(rest_key, (tile_total, TOPM - CAP), 0, span_count - 1)
    others = others + (others >= busy[:, None]).astype(jnp.int32)
    offsets = jnp.concatenate([jnp.broadcast_to(busy[:, None], (tile_total, CAP)), others], axis=1)
    earlier = jnp.arange(TOPM)[None, :] < jnp.arange(TOPM)[:, None]
    same_owner = (offsets[:, :, None] == offsets[:, None, :]) & earlier[None, :, :]
    ranks = jnp.sum(same_owner.astype(jnp.int32), axis=2)
    perm_keys = jax.random.split(perm_key, tile_total * span_count)
    perms = jax.vmap(lambda one_key: jax.random.permutation(one_key, MEM_DEV))(perm_keys)
    perms = perms.reshape(tile_total, span_count * MEM_DEV).astype(jnp.int32)
    slots = jnp.take_along_axis(perms, offsets * MEM_DEV + ranks, axis=1)
    sector = (jnp.arange(tile_total) % N_LON)[:, None]
    owner = (sector + offsets - REACH) % N_LON
    return (owner * MEM_DEV + slots).astype(jnp.int32).reshape(N_LAT, N_LON, TOPM)


def draw_memory_count(key, part):
    key = jax.random.fold_in(key, 6)
    count_key, pick_key, short_key = jax.random.split(key, 3)
    tile_total = N_LAT * N_LON
    counts = jax.random.randint(count_key, (tile_total,), TOPM - 1, TOPM + 1)
    chosen = jax.random.randint(pick_key, (), 0, tile_total)
    short_one = (chosen + 1 + jax.random.randint(short_key, (), 0, tile_total - 1)) % tile_total
    counts = jnp.where(jnp.arange(tile_total) == chosen, TOPM, counts)
    counts = jnp.where(jnp.arange(tile_total) == short_one, TOPM - 1, counts)
    return counts.astype(jnp.int32).reshape(N_LAT, N_LON)


def levels(own_key, shape, shards, low, high):
    def one(position, shards_of):
        steps = jax.random.uniform(jax.random.fold_in(jax.random.fold_in(own_key, 6), position), (shards_of,), jnp.float32, low / len(shards), high / len(shards))
        return jnp.repeat(jnp.exp(steps), shape[position] // shards_of).reshape((-1,) + (1,) * (len(shape) - position - 1))

    loudness = one(*shards[0])
    for cut in shards[1:]:
        loudness = loudness * one(*cut)
    return loudness


def noise(own_key, extent, spread, limit, pieces=(), kind=jnp.bfloat16):
    values = spread * jax.random.normal(own_key, extent, jnp.float32)
    if pieces:
        values = values * levels(own_key, extent, pieces, -0.22, 0.18)
    return jnp.clip(values, -limit, limit).astype(kind)


def setup_inputs(seed: int = 0) -> dict:
    keys = jax.random.split(jax.random.key(seed), 7)
    return {
        "queries": draw_queries(jax.random.fold_in(keys[6], 71), 0),
        "token_keys": draw_token_keys(jax.random.fold_in(keys[6], 71), 0),
        "token_values": noise(keys[2], (FRAMES, LAT, LON, HEADS * HEAD_DIM), 1.0, 6.0, ((1, 4), (2, 64))),
        "memory_bank": draw_memory_bank(jax.random.fold_in(keys[6], 71), 0),
        "memory_ids": draw_memory_ids(jax.random.fold_in(keys[6], 71), 0),
        "memory_count": draw_memory_count(jax.random.fold_in(keys[6], 71), 0),
    }


MASKED = -1e30


def attend(query_rows, key_rows, value_rows, valid):
    count_q = query_rows.shape[0]
    q3 = query_rows.astype(jnp.float32).reshape(count_q, HEADS, HEAD_DIM)
    k3 = key_rows.astype(jnp.float32).reshape(key_rows.shape[0], HEADS, HEAD_DIM)
    v3 = value_rows.astype(jnp.float32).reshape(value_rows.shape[0], HEADS, HEAD_DIM)
    scores = jnp.einsum("qhd,khd->hqk", q3, k3) * (HEAD_DIM ** -0.5)
    scores = jnp.where(valid[None, None, :], scores, MASKED)
    largest = jnp.max(scores, axis=2, keepdims=True)
    weights = jnp.exp(scores - largest)
    totals = jnp.sum(weights, axis=2)
    rounded = lax.optimization_barrier(weights.astype(jnp.bfloat16)).astype(jnp.float32)
    mixture = jnp.einsum("hqk,khd->qhd", rounded, v3) / jnp.transpose(totals)[:, :, None]
    return mixture.reshape(count_q, HEADS * HEAD_DIM)


def reference(queries, token_keys, token_values, memory_bank, memory_ids, memory_count):
    feature_width = HEADS * HEAD_DIM
    block_tokens = LAT_DEV * LON_DEV
    key_value = jnp.stack([token_keys, token_values])
    key_value = jnp.concatenate([key_value[:, :, :, LON - LON_DEV:], key_value, key_value[:, :, :, :LON_DEV]], axis=3)
    key_value = jnp.pad(key_value, ((0, 0), (0, 0), (LAT_DEV, LAT_DEV), (0, 0), (0, 0)))
    row_flags = jnp.pad(jnp.ones((LAT,), jnp.int32), (LAT_DEV, LAT_DEV))
    zero_index = jnp.int32(0)

    def one_tile(tile_index):
        band_index = (tile_index // N_LON).astype(jnp.int32)
        sector = (tile_index % N_LON).astype(jnp.int32)
        lat_start = (band_index * LAT_DEV).astype(jnp.int32)
        lon_start = (sector * LON_DEV).astype(jnp.int32)
        tile_queries = lax.dynamic_slice(queries, (zero_index, lat_start, lon_start, zero_index), (FRAMES, LAT_DEV, LON_DEV, feature_width))
        tile_queries = tile_queries.reshape(-1, feature_width)
        region = lax.dynamic_slice(key_value, (zero_index, zero_index, lat_start, lon_start, zero_index), (2, FRAMES, 3 * LAT_DEV, 3 * LON_DEV, feature_width))
        row_valid = lax.dynamic_slice(row_flags, (lat_start,), (3 * LAT_DEV,)) > 0
        near_valid = jnp.broadcast_to(row_valid[None, :, None], (FRAMES, 3 * LAT_DEV, 3 * LON_DEV)).reshape(-1)
        near_out = attend(tile_queries, region[0].reshape(-1, feature_width), region[1].reshape(-1, feature_width), near_valid)
        entry_ids = memory_ids[band_index, sector]
        live_count = memory_count[band_index, sector]
        owner_col = (entry_ids // MEM_DEV).astype(jnp.int32)
        slot_index = (entry_ids % MEM_DEV).astype(jnp.int32)

        def fetch(owner_one, slot_one):
            return lax.dynamic_slice(memory_bank, (zero_index, slot_one, lat_start, (owner_one * LON_DEV).astype(jnp.int32), zero_index), (2, 1, LAT_DEV, LON_DEV, feature_width))

        blocks_all = jax.vmap(fetch)(owner_col, slot_index)
        memory_keys = blocks_all[:, 0].reshape(-1, feature_width)
        memory_values = blocks_all[:, 1].reshape(-1, feature_width)
        live_entry = jnp.arange(TOPM, dtype=jnp.int32) < live_count
        far_valid = jnp.repeat(live_entry, block_tokens)
        far_out = attend(tile_queries, memory_keys, memory_values, far_valid)
        return (near_out + far_out).astype(jnp.bfloat16).reshape(FRAMES, LAT_DEV, LON_DEV, feature_width)

    tiles_out = lax.map(one_tile, jnp.arange(N_LAT * N_LON, dtype=jnp.int32))
    tiles_out = tiles_out.reshape(N_LAT, N_LON, FRAMES, LAT_DEV, LON_DEV, feature_width)
    tiles_out = jnp.transpose(tiles_out, (2, 0, 3, 1, 4, 5))
    return tiles_out.reshape(FRAMES, LAT, LON, feature_width)
```

```python
import functools

import jax
import jax.numpy as jnp
from jax import lax
from jax.experimental import pallas as pl
from jax.experimental.pallas import tpu as pltpu
from jax.sharding import PartitionSpec as P

HEAD_DIM = 128
REACH = 2
MASKED = -1e30
FLOOR = -30000.0
SCALE2 = HEAD_DIM ** (-0.5) * 1.4426950408889634
FAR_LANE = 36
LOW_LANE = 12
EXP_LANE = 24
STAT = 128
CODE_ROWS = 16

VMEM = pl.BlockSpec(memory_space=pltpu.VMEM)
SMEM = pl.BlockSpec(memory_space=pltpu.SMEM)
ANY = pl.BlockSpec(memory_space=pl.ANY)
PARAMS = pltpu.CompilerParams(vmem_limit_bytes=48 * 1024 * 1024)


def call(body, out_shape, in_specs, *operands):
    single = not isinstance(out_shape, (list, tuple))
    return pl.pallas_call(
        body,
        out_shape=out_shape,
        in_specs=in_specs,
        out_specs=VMEM if single else [VMEM] * len(out_shape),
        compiler_params=PARAMS,
    )(*operands)


def columns(head):
    return pl.ds(head * HEAD_DIM, HEAD_DIM)


def dot_t(a, b):
    return lax.dot_general(a, b, (((1,), (1,)), ((), ())), preferred_element_type=jnp.float32)


def prep_queries(q_ref, ids_ref, count_ref, out_ref, *, slots, sectors):
    rows = q_ref.shape[0] * q_ref.shape[1] * q_ref.shape[2]
    width = q_ref.shape[3]
    out_ref[:rows, :] = q_ref[...].reshape(rows, width)
    sector = lax.axis_index("lon")
    block = q_ref.shape[1] * q_ref.shape[2]
    lane_code = lax.broadcasted_iota(jnp.int32, (CODE_ROWS, width), 1) // block
    live = count_ref[0, 0]
    bias = jnp.full((CODE_ROWS, width), MASKED, jnp.float32)
    for e in range(ids_ref.shape[2]):
        entry = ids_ref[0, 0, e]
        owner = entry // slots
        offset = lax.rem(owner - sector + REACH + sectors, sectors)
        code = jnp.where(e < live, offset * slots + entry % slots, -1)
        bias = jnp.where(lane_code == code, 0.0, bias)
    out_ref[rows:, :] = bias.astype(jnp.bfloat16)


def prep_pair(k_ref, v_ref, out_ref):
    rows = out_ref.shape[0] // 2
    out_ref[:rows, :] = k_ref[...].reshape(rows, out_ref.shape[1])
    out_ref[rows:, :] = v_ref[...].reshape(rows, out_ref.shape[1])


def prep_bank(bank_ref, out_ref):
    out_ref[...] = bank_ref[...].reshape(out_ref.shape)


def softmax_part(scores, values):
    largest = jnp.max(scores, axis=1, keepdims=True)
    weights = jnp.exp2((scores - largest) * SCALE2)
    total = jnp.sum(weights, axis=1, keepdims=True)
    mixed = jnp.dot(weights.astype(jnp.bfloat16), values, preferred_element_type=jnp.float32)
    level = jnp.maximum(largest * SCALE2 + jnp.log2(total), FLOOR)
    return mixed * (1.0 / total), level


def near_part(queries, tiles, head):
    band = lax.axis_index("lat")
    bands = lax.axis_size("lat")
    rows = tiles[0].shape[0] // 2
    shut = (
        None,
        jnp.where(band > 0, 0.0, MASKED).astype(jnp.float32),
        jnp.where(band < bands - 1, 0.0, MASKED).astype(jnp.float32),
    )
    scores, values = [], []
    for tile, closed in zip(tiles, shut):
        part = dot_t(queries, tile[:rows, columns(head)])
        scores.append(part if closed is None else part + closed)
        values.append(tile[rows:, columns(head)])
    return softmax_part(jnp.concatenate(scores, axis=1), jnp.concatenate(values, axis=0))


def far_part(queries, biases, bank, head):
    rows = bank.shape[0] // 2
    scores = dot_t(queries, bank[:rows, columns(head)])
    each = scores.shape[0] // len(biases)
    scores = jnp.concatenate(
        [scores[i * each : (i + 1) * each] + bias for i, bias in enumerate(biases)], axis=0
    )
    return softmax_part(scores, bank[rows:, columns(head)])


def mask_of(q_ref, offset, keys):
    rows = q_ref.shape[0] - CODE_ROWS
    return q_ref[rows:, pl.ds((offset + REACH) * keys, keys)].astype(jnp.float32)[:1]


def put_coded(out_ref, stats, lanes, mixed, level, column, lane):
    peak = jnp.max(jnp.abs(mixed), axis=1, keepdims=True)
    power = jnp.ceil(jnp.log2(jnp.maximum(peak, 1e-30)))
    out_ref[:, columns(column)] = jnp.round(mixed * jnp.exp2(14.0 - power)).astype(jnp.int32).astype(jnp.int16)
    whole = jnp.floor(level)
    low = jnp.minimum(jnp.floor((level - whole) * 32768.0), 32767.0)
    stats = jnp.where(lanes == lane, whole, stats)
    stats = jnp.where(lanes == lane + LOW_LANE, low, stats)
    return jnp.where(lanes == lane + EXP_LANE, power, stats)


def part_near_far(low_ref, high_ref, own_ref, up_ref, down_ref, bank_ref, low_out, high_out):
    rows = low_out.shape[0]
    heads = own_ref.shape[1] // HEAD_DIM
    keys = bank_ref.shape[0] // 2
    lanes = lax.broadcasted_iota(jnp.int32, (rows, STAT), 1)
    biases = [mask_of(low_ref, 1, keys), mask_of(high_ref, -1, keys)]
    outs = (low_out, high_out)
    stats = [jnp.zeros((rows, STAT), jnp.float32) for _ in outs]
    for head in range(heads):
        queries = jnp.concatenate([low_ref[:rows, columns(head)], high_ref[:rows, columns(head)]], axis=0)
        near, near_level = near_part(queries, (own_ref, up_ref, down_ref), head)
        far, far_level = far_part(queries, biases, bank_ref, head)
        for i, out in enumerate(outs):
            cut = slice(i * rows, (i + 1) * rows)
            stats[i] = put_coded(out, stats[i], lanes, near[cut], near_level[cut], head, head)
            stats[i] = put_coded(
                out, stats[i], lanes, far[cut], far_level[cut], heads + head, FAR_LANE + head
            )
    for out, stat in zip(outs, stats):
        out[:, 2 * heads * HEAD_DIM :] = stat.astype(jnp.int32).astype(jnp.int16)


def part_far(low_ref, high_ref, bank_ref, low_out, high_out):
    rows = low_out.shape[0]
    heads = bank_ref.shape[1] // HEAD_DIM
    keys = bank_ref.shape[0] // 2
    lanes = lax.broadcasted_iota(jnp.int32, (rows, STAT), 1)
    biases = [mask_of(low_ref, 2, keys), mask_of(high_ref, -2, keys)]
    outs = (low_out, high_out)
    stats = [jnp.where(lanes < FAR_LANE, FLOOR, 0.0) for _ in outs]
    for head in range(heads):
        queries = jnp.concatenate([low_ref[:rows, columns(head)], high_ref[:rows, columns(head)]], axis=0)
        far, far_level = far_part(queries, biases, bank_ref, head)
        for i, out in enumerate(outs):
            cut = slice(i * rows, (i + 1) * rows)
            stats[i] = put_coded(out, stats[i], lanes, far[cut], far_level[cut], head, FAR_LANE + head)
    for out, stat in zip(outs, stats):
        out[:, heads * HEAD_DIM :] = stat.astype(jnp.int32).astype(jnp.int16)


def part_own(q_ref, own_ref, up_ref, down_ref, bank_ref, _after, near_out, far_out, level_out):
    rows = near_out.shape[0]
    heads = own_ref.shape[1] // HEAD_DIM
    keys = bank_ref.shape[0] // 2
    lanes = lax.broadcasted_iota(jnp.int32, (rows, STAT), 1)
    bias = mask_of(q_ref, 0, keys)
    levels = jnp.full((rows, STAT), FLOOR, jnp.float32)
    for head in range(heads):
        queries = q_ref[:rows, columns(head)]
        near, near_level = near_part(queries, (own_ref, up_ref, down_ref), head)
        far, far_level = far_part(queries, [bias], bank_ref, head)
        near_out[:, columns(head)] = near
        far_out[:, columns(head)] = far
        levels = jnp.where(lanes == head, near_level, levels)
        levels = jnp.where(lanes == FAR_LANE + head, far_level, levels)
    level_out[...] = levels


def merge(near_ref, far_ref, level_ref, one_low, one_high, two_low, two_high, out_ref):
    rows, width = near_ref.shape
    heads = width // HEAD_DIM
    near_far = (one_low, one_high)
    far_only = (two_low, two_high)
    levels, factors = [level_ref[...]], [None]
    for ref in near_far + far_only:
        stat = ref[:, ref.shape[1] - STAT :].astype(jnp.int32).astype(jnp.float32)
        low = pltpu.roll(stat, STAT - LOW_LANE, 1)
        power = pltpu.roll(stat, STAT - EXP_LANE, 1)
        levels.append(stat + low * (1.0 / 32768.0))
        factors.append(jnp.exp2(power - 14.0))
    lanes = lax.broadcasted_iota(jnp.int32, (rows, STAT), 1)
    for i in (3, 4):
        levels[i] = jnp.where(lanes < FAR_LANE, FLOOR, levels[i])
    largest = functools.reduce(jnp.maximum, levels)
    weights = [jnp.exp2(level - largest) for level in levels]
    inverse = 1.0 / functools.reduce(jnp.add, weights)
    shares = [w * inverse if f is None else w * inverse * f for w, f in zip(weights, factors)]

    def decoded(ref, column):
        return ref[:, columns(column)].astype(jnp.int32).astype(jnp.float32)

    for head in range(heads):
        near, far = slice(head, head + 1), slice(FAR_LANE + head, FAR_LANE + head + 1)
        total = near_ref[:, columns(head)] * shares[0][:, near] + far_ref[:, columns(head)] * shares[0][:, far]
        for ref, share in zip(near_far, shares[1:3]):
            total += decoded(ref, head) * share[:, near] + decoded(ref, heads + head) * share[:, far]
        for ref, share in zip(far_only, shares[3:]):
            total += decoded(ref, head) * share[:, far]
        out_ref[:, :, :, columns(head)] = total.astype(jnp.bfloat16).reshape(out_ref.shape[:3] + (HEAD_DIM,))


def around(value, steps):
    count = lax.axis_size("lon")
    return lax.ppermute(value, "lon", [(i, (i + steps) % count) for i in range(count)])


def along(value, steps):
    count = lax.axis_size("lat")
    return lax.ppermute(
        value, "lat", [(i, i + steps) for i in range(count) if 0 <= i + steps < count]
    )


def local(queries, token_keys, token_values, memory_bank, memory_ids, memory_count):
    frames, band_rows, tile_cols, width = queries.shape
    rows = frames * band_rows * tile_cols
    slots = memory_bank.shape[1]
    sectors = lax.axis_size("lon")
    shape = jax.ShapeDtypeStruct

    coded_queries = call(
        functools.partial(prep_queries, slots=slots, sectors=sectors),
        shape((rows + CODE_ROWS, width), jnp.bfloat16),
        [VMEM, SMEM, SMEM],
        queries, memory_ids, memory_count,
    )
    one_low, one_high = around(coded_queries, 1), around(coded_queries, -1)
    pair = call(prep_pair, shape((2 * rows, width), jnp.bfloat16), [VMEM, VMEM], token_keys, token_values)
    up, down = along(pair, 1), along(pair, -1)
    bank = call(
        prep_bank,
        shape((2 * slots * band_rows * tile_cols, width), jnp.bfloat16),
        [VMEM], memory_bank,
    )
    two_low, two_high = around(one_low, 1), around(one_high, -1)
    both = shape((rows, 2 * width + STAT), jnp.int16)
    single = shape((rows, width + STAT), jnp.int16)
    one_low_out, one_high_out = call(
        part_near_far, [both, both], [VMEM] * 6, one_low, one_high, pair, up, down, bank
    )
    back_one_high = around(one_low_out, -1)
    back_one_low = around(one_high_out, 1)
    two_low_out, two_high_out = call(part_far, [single, single], [VMEM] * 3, two_low, two_high, bank)
    back_two_high = around(two_low_out, -2)
    back_two_low = around(two_high_out, 2)
    near, far, level = call(
        part_own,
        [shape((rows, width), jnp.float32)] * 2 + [shape((rows, STAT), jnp.float32)],
        [VMEM] * 5 + [ANY],
        coded_queries, pair, up, down, bank, two_low_out,
    )
    return call(
        merge, shape(queries.shape, jnp.bfloat16), [VMEM] * 7,
        near, far, level, back_one_low, back_one_high, back_two_low, back_two_high,
    )


def solution(mesh):
    placed = (
        P(None, "lat", "lon", None),
        P(None, "lat", "lon", None),
        P(None, "lat", "lon", None),
        P(None, None, "lat", "lon", None),
        P("lat", "lon", None),
        P("lat", "lon"),
    )
    return jax.shard_map(
        local, mesh=mesh, in_specs=placed, out_specs=P(None, "lat", "lon", None), check_vma=False
    )
```

```python
import functools

import jax
import jax.numpy as jnp
from jax import lax
from jax.experimental import pallas as pl
from jax.experimental.pallas import tpu as pltpu
from jax.sharding import PartitionSpec as P

HEAD_DIM = 128
REACH = 2
CAP = 4
MASKED = -1e30
FLOOR = -30000.0
SCALE2 = HEAD_DIM ** (-0.5) * 1.4426950408889634
FAR_LANE = 64
LOW_LANE = 12
EXP_LANE = 24
STAT = 128
CODE_ROWS = 16
ROUNDER = 12582912.0

VMEM = pl.BlockSpec(memory_space=pltpu.VMEM)
SMEM = pl.BlockSpec(memory_space=pltpu.SMEM)
ANY = pl.BlockSpec(memory_space=pl.ANY)
PARAMS = pltpu.CompilerParams(vmem_limit_bytes=48 * 1024 * 1024)


def call(body, out_shape, in_specs, *operands, scratch=()):
    single = not isinstance(out_shape, (list, tuple))
    return pl.pallas_call(
        body,
        out_shape=out_shape,
        in_specs=in_specs,
        out_specs=VMEM if single else [VMEM] * len(out_shape),
        scratch_shapes=list(scratch),
        compiler_params=PARAMS,
    )(*operands)


def columns(head):
    return pl.ds(head * HEAD_DIM, HEAD_DIM)


def dot_t(a, b):
    return lax.dot_general(a, b, (((1,), (1,)), ((), ())), preferred_element_type=jnp.float32)


def prep_queries(q_ref, ids_ref, out_ref, *, slots, sectors):
    rows = q_ref.shape[0] * q_ref.shape[1] * q_ref.shape[2]
    width = q_ref.shape[3]
    out_ref[:rows, :] = q_ref[...].reshape(rows, width)
    sector = lax.axis_index("lon")
    block = q_ref.shape[1] * q_ref.shape[2]
    lane_code = lax.broadcasted_iota(jnp.int32, (CODE_ROWS, width), 1) // block
    bias = jnp.full((CODE_ROWS, width), MASKED, jnp.float32)
    used = [jnp.int32(0), jnp.int32(0)]
    for e in range(ids_ref.shape[0]):
        entry = ids_ref[e]
        offset = lax.rem(entry // slots - sector + REACH + sectors, sectors)
        place = entry % slots
        for i, far_end in enumerate((0, 2 * REACH)):
            there = (offset == far_end) & (entry >= 0)
            place = jnp.where(offset == far_end, used[i], place)
            used[i] = used[i] + there.astype(jnp.int32)
        code = jnp.where(entry >= 0, offset * slots + place, -1)
        bias = jnp.where(lane_code == code, 0.0, bias)
    out_ref[rows:, :] = bias.astype(jnp.bfloat16)


def pack_blocks(bank_ref, first_ref, second_ref, outs, slots):
    rows = bank_ref.shape[0] // 2
    block = rows // slots
    sector = lax.axis_index("lon")
    straight = side_of(1) == side_of(REACH)
    for (mine_ref, cross_ref), out in zip(((first_ref, second_ref), (second_ref, first_ref)), outs):
        picks = [jnp.int32(0)] * CAP
        used = jnp.int32(0)
        for e in range(first_ref.shape[0]):
            entry = jnp.where(straight, mine_ref[e], cross_ref[e])
            named = (entry >= 0) & (entry // slots == sector)
            for p in range(CAP):
                picks[p] = jnp.where(named & (used == p), entry % slots, picks[p])
            used = used + named.astype(jnp.int32)
        for half in range(2):
            for p in range(CAP):
                start = pl.multiple_of(half * rows + picks[p] * block, block)
                out[pl.ds((half * CAP + p) * block, block), :] = bank_ref[pl.ds(start, block), :]


def prep_pair(k_ref, v_ref, _after, out_ref):
    rows = out_ref.shape[0] // 2
    out_ref[:rows, :] = k_ref[...].reshape(rows, out_ref.shape[1])
    out_ref[rows:, :] = v_ref[...].reshape(rows, out_ref.shape[1])


def prep_bank(bank_ref, out_ref):
    out_ref[...] = bank_ref[...].reshape(out_ref.shape)


def prep_packs(bank_ref, first_ref, second_ref, _one, _two, a_out, b_out, *, slots):
    pack_blocks(bank_ref, first_ref, second_ref, (a_out, b_out), slots)


def softmax_part(scores, values):
    largest = jnp.max(scores, axis=1, keepdims=True)
    weights = jnp.exp2((scores - largest) * SCALE2)
    total = jnp.sum(weights, axis=1, keepdims=True)
    mixed = jnp.dot(weights.astype(jnp.bfloat16), values, preferred_element_type=jnp.float32)
    return mixed, jnp.maximum(largest * SCALE2, FLOOR), total


def near_part(queries, tiles, head):
    band = lax.axis_index("lat")
    bands = lax.axis_size("lat")
    rows = tiles[0].shape[0] // 2
    meets = (band % 2 == 1) & (band < bands - 1) | (band % 2 == 0) & (band > 0)
    shut = jnp.where(meets, 0.0, MASKED).astype(jnp.float32)
    scores = [dot_t(queries, tile[:rows, columns(head)]) for tile in tiles]
    scores[2] = scores[2] + shut
    values = [tile[rows:, columns(head)] for tile in tiles]
    return softmax_part(jnp.concatenate(scores, axis=1), jnp.concatenate(values, axis=0))


def far_part(queries, ref, bias, head):
    rows = ref.shape[0] // 2
    scores = dot_t(queries, ref[:rows, columns(head)]) + bias
    return softmax_part(scores, ref[rows:, columns(head)])


def mask_of(q_ref, offset, keys, stride):
    rows = q_ref.shape[0] - CODE_ROWS
    return q_ref[rows:, pl.ds((offset + REACH) * stride, keys)].astype(jnp.float32)[:1]


def mask_for(q_ref, index, distance, keys, stride):
    down, up = (mask_of(q_ref, x, keys, stride) for x in (-distance, distance))
    above = (side_of() > 0) if index == 0 else (side_of() < 0)
    return jnp.where(above, down, up)


def lanes_of(rows):
    return lax.broadcasted_iota(jnp.int32, (rows, STAT), 1)


def peak_of(mixed):
    return jnp.max(jnp.abs(mixed), axis=1, keepdims=True)


def power_of(peak):
    return jnp.ceil(jnp.log2(jnp.maximum(peak, 1e-30)))


def put_code(out_ref, values, head):
    out_ref[:, columns(head)] = ((values + ROUNDER) - ROUNDER).astype(jnp.int32).astype(jnp.int16)


def coded_stats(level, power, heads):
    live = lanes_of(level.shape[0]) < heads
    whole = jnp.floor(level)
    low = jnp.minimum(jnp.floor((level - whole) * 32768.0), 32767.0)
    whole, low, power = (jnp.where(live, x, 0.0) for x in (whole, low, power))
    return whole + pltpu.roll(low, LOW_LANE, 1) + pltpu.roll(power, EXP_LANE, 1)


def put_stats(out_ref, stats):
    out_ref[:, out_ref.shape[1] - STAT :] = stats.astype(jnp.int32).astype(jnp.int16)


def near_sides(a_ref, b_ref, own_ref, mate_ref, other_ref, _after, a_out, b_out, a_mix, b_mix):
    rows = a_out.shape[0]
    heads = own_ref.shape[1] // HEAD_DIM
    lanes = lanes_of(rows)
    sides = ((a_out, a_mix), (b_out, b_mix))
    tops, totals, peaks = ([jnp.ones((rows, STAT), jnp.float32) for _ in sides] for _ in range(3))
    for head in range(heads):
        queries = jnp.concatenate([a_ref[:rows, columns(head)], b_ref[:rows, columns(head)]], axis=0)
        mixed, top, total = near_part(queries, (own_ref, mate_ref, other_ref), head)
        peak = peak_of(mixed)
        for i, (_, mix) in enumerate(sides):
            cut = slice(i * rows, (i + 1) * rows)
            mix[:, columns(head)] = mixed[cut]
            tops[i] = jnp.where(lanes == head, top[cut], tops[i])
            totals[i] = jnp.where(lanes == head, total[cut], totals[i])
            peaks[i] = jnp.where(lanes == head, peak[cut], peaks[i])
    for (out, mix), top, total, peak in zip(sides, tops, totals, peaks):
        inverse = 1.0 / total
        power = power_of(peak * inverse)
        scale = inverse * jnp.exp2(14.0 - power)
        put_stats(out, coded_stats(jnp.maximum(top + jnp.log2(total), FLOOR), power, heads))
        for head in range(heads):
            put_code(out, mix[:, columns(head)] * scale[:, head : head + 1], head)


def far_sides(a_ref, b_ref, bank_ref, _after, a_mix, b_mix, a_stat, b_stat):
    rows = a_mix.shape[0]
    keys = bank_ref.shape[0] // 2
    lanes = lanes_of(rows)
    for index, (ref, mix, stat) in enumerate(((a_ref, a_mix, a_stat), (b_ref, b_mix, b_stat))):
        bias = mask_for(ref, index, 1, keys, keys)
        packed = [jnp.zeros((rows, STAT), jnp.float32) for _ in range(3)]
        for head in range(bank_ref.shape[1] // HEAD_DIM):
            mixed, top, total = far_part(ref[:rows, columns(head)], bank_ref, bias, head)
            mix[:, columns(head)] = mixed
            packed = [
                jnp.where(lanes == head, x, p) for x, p in zip((top, total, peak_of(mixed)), packed)
            ]
        for i, p in enumerate(packed):
            stat[:, i * STAT : (i + 1) * STAT] = p


def far_beyond(
    a_ref, b_ref, a_part, b_part, a_stat, b_stat, a_pack, b_pack, a_out, b_out, mix, *, keys
):
    rows, width = a_part.shape
    heads = width // HEAD_DIM
    packed = a_pack.shape[0] // 2
    masks = [mask_for(ref, index, 2, packed, keys) for index, ref in enumerate((a_ref, b_ref))]
    masks = [jnp.broadcast_to(mask, (rows, packed)) for mask in masks]
    closed = jnp.full((rows, packed), MASKED, jnp.float32)
    bias = jnp.concatenate(
        [jnp.concatenate([masks[0], closed], axis=1), jnp.concatenate([closed, masks[1]], axis=1)], axis=0
    )
    lanes = lanes_of(2 * rows)
    news = [jnp.zeros((2 * rows, STAT), jnp.float32) for _ in range(3)]
    for head in range(heads):
        cut = columns(head)
        queries = jnp.concatenate([a_ref[:rows, cut], b_ref[:rows, cut]], axis=0)
        far_keys = jnp.concatenate([b_pack[:packed, cut], a_pack[:packed, cut]], axis=0)
        far_values = jnp.concatenate([b_pack[packed:, cut], a_pack[packed:, cut]], axis=0)
        mixed, top, total = softmax_part(dot_t(queries, far_keys) + bias, far_values)
        mix[:, cut] = mixed
        news = [jnp.where(lanes == head, x, p) for x, p in zip((top, total, peak_of(mixed)), news)]
    lanes = lanes_of(rows)
    for index, (part, stat, out) in enumerate(((a_part, a_stat, a_out), (b_part, b_stat, b_out))):
        half = slice(index * rows, (index + 1) * rows)
        new = [x[half] for x in news]
        olds = [stat[:, i * STAT : (i + 1) * STAT] for i in range(3)]
        largest = jnp.maximum(olds[0], new[0])
        old_share, new_share = jnp.exp2(olds[0] - largest), jnp.exp2(new[0] - largest)
        total = jnp.where(lanes < heads, olds[1] * old_share + new[1] * new_share, 1.0)
        inverse = 1.0 / total
        old_share, new_share = old_share * inverse, new_share * inverse
        power = power_of(olds[2] * old_share + new[2] * new_share)
        scale = jnp.exp2(14.0 - power)
        old_share, new_share = old_share * scale, new_share * scale
        put_stats(out, coded_stats(jnp.maximum(largest + jnp.log2(total), FLOOR), power, heads))
        for head in range(heads):
            one, cut = slice(head, head + 1), columns(head)
            put_code(out, part[:, cut] * old_share[:, one] + mix[half, cut] * new_share[:, one], head)


def part_own(q_ref, own_ref, mate_ref, other_ref, bank_ref, near_out, far_out, stat_out):
    rows = near_out.shape[0]
    keys = bank_ref.shape[0] // 2
    lanes = lanes_of(rows)
    bias = mask_of(q_ref, 0, keys, keys)
    tops = jnp.full((rows, STAT), FLOOR, jnp.float32)
    totals = jnp.ones((rows, STAT), jnp.float32)
    for head in range(own_ref.shape[1] // HEAD_DIM):
        queries = q_ref[:rows, columns(head)]
        for mixed, top, total, out, lane in (
            near_part(queries, (own_ref, mate_ref, other_ref), head) + (near_out, head),
            far_part(queries, bank_ref, bias, head) + (far_out, FAR_LANE + head),
        ):
            out[:, columns(head)] = mixed
            tops = jnp.where(lanes == lane, top, tops)
            totals = jnp.where(lanes == lane, total, totals)
    stat_out[:, :STAT] = jnp.maximum(tops + jnp.log2(totals), FLOOR)
    stat_out[:, STAT:] = 1.0 / totals


def merge(near_ref, far_ref, own_ref, a_near, b_near, a_far, b_far, out_ref):
    width = near_ref.shape[1]
    sides = ((a_near, a_far), (b_near, b_far))
    levels, factors = [own_ref[:, :STAT]], [own_ref[:, STAT:]]
    for refs in sides:
        near, far = (ref[:, width:].astype(jnp.int32).astype(jnp.float32) for ref in refs)
        stat = near + pltpu.roll(far, FAR_LANE, 1)
        low = pltpu.roll(stat, STAT - LOW_LANE, 1)
        power = pltpu.roll(stat, STAT - EXP_LANE, 1)
        levels.append(stat + low * (1.0 / 32768.0))
        factors.append(jnp.exp2(power - 14.0))
    largest = functools.reduce(jnp.maximum, levels)
    weights = [jnp.exp2(level - largest) for level in levels]
    inverse = 1.0 / functools.reduce(jnp.add, weights)
    shares = [w * inverse * f for w, f in zip(weights, factors)]
    for head in range(width // HEAD_DIM):
        lanes = (slice(head, head + 1), slice(FAR_LANE + head, FAR_LANE + head + 1))
        total = sum(ref[:, columns(head)] * shares[0][:, lane] for ref, lane in zip((near_ref, far_ref), lanes))
        for refs, share in zip(sides, shares[1:]):
            for ref, lane in zip(refs, lanes):
                total += ref[:, columns(head)].astype(jnp.int32).astype(jnp.float32) * share[:, lane]
        out_ref[:, :, :, columns(head)] = total.astype(jnp.bfloat16).reshape(out_ref.shape[:3] + (HEAD_DIM,))


def swapped(value, first, axis="lon", reach=1, closed=True):
    count = lax.axis_size(axis)
    pairs = []
    for i in range(count):
        up = (i // reach) % 2 == first
        partner = i + reach if up else i - reach
        if closed or 0 <= partner < count:
            pairs.append((i, partner % count))
    return lax.ppermute(value, axis, pairs)


def side_of(reach=1):
    return 1 - 2 * ((lax.axis_index("lon") // reach) % 2)


def local(queries, token_keys, token_values, memory_bank, memory_ids, memory_count):
    frames, band_rows, tile_cols, width = queries.shape
    rows = frames * band_rows * tile_cols
    slots = memory_bank.shape[1]
    sectors = lax.axis_size("lon")
    shape = jax.ShapeDtypeStruct

    entries = memory_ids.reshape(-1)
    wanted = jnp.where(jnp.arange(entries.shape[0]) < memory_count.reshape(()), entries, -1)
    block = band_rows * tile_cols
    keys = slots * block
    bank = call(prep_bank, shape((2 * keys, width), jnp.bfloat16), [VMEM], memory_bank)
    packs = shape((2 * CAP * block, width), jnp.bfloat16)
    queries_shape = shape((rows + CODE_ROWS, width), jnp.bfloat16)
    first, second = swapped(wanted, 0, reach=REACH), swapped(wanted, 1, reach=REACH)
    coded_queries = call(
        functools.partial(prep_queries, slots=slots, sectors=sectors), queries_shape, [VMEM, SMEM], queries, wanted
    )
    q_b, q_a = swapped(coded_queries, 1), swapped(coded_queries, 0)
    pack_a, pack_b = call(
        functools.partial(prep_packs, slots=slots), [packs, packs], [VMEM, SMEM, SMEM, ANY, ANY],
        bank, first, second, q_a, q_b,
    )
    from_b, from_a = swapped(pack_b, 1), swapped(pack_a, 0)
    pair = call(
        prep_pair, shape((2 * rows, width), jnp.bfloat16), [VMEM, VMEM, ANY],
        token_keys, token_values, coded_queries,
    )
    other = swapped(pair, 1, "lat", closed=False)
    late = call(
        prep_pair, shape((2 * rows, width), jnp.bfloat16), [VMEM, VMEM, ANY],
        token_keys, token_values, first,
    )
    mate = swapped(late, 0, "lat", closed=False)
    plain = shape((rows, width), jnp.float32)
    work = pltpu.VMEM((rows, width), jnp.float32)
    near, far, own_stat = call(
        part_own, [plain, plain, shape((rows, 2 * STAT), jnp.float32)], [VMEM] * 5,
        coded_queries, pair, mate, other, bank,
    )
    coded = [shape((rows, width + STAT), jnp.int16)] * 2
    a_near, b_near = call(
        near_sides, coded, [VMEM] * 5 + [ANY], q_a, q_b, pair, mate, other, own_stat, scratch=[work, work]
    )
    back_b_near, back_a_near = swapped(b_near, 1), swapped(a_near, 0)
    stats = shape((rows, 3 * STAT), jnp.float32)
    a_far, b_far, a_stat, b_stat = call(
        far_sides, [plain, plain, stats, stats], [VMEM] * 3 + [ANY], q_a, q_b, bank, a_near
    )
    a_far, b_far = call(
        functools.partial(far_beyond, keys=keys), coded, [VMEM] * 8,
        q_a, q_b, a_far, b_far, a_stat, b_stat, from_a, from_b, scratch=[pltpu.VMEM((2 * rows, width), jnp.float32)],
    )
    back_b_far, back_a_far = swapped(b_far, 1), swapped(a_far, 0)
    return call(
        merge, shape(queries.shape, jnp.bfloat16), [VMEM] * 7,
        near, far, own_stat, back_a_near, back_b_near, back_a_far, back_b_far,
    )


def solution(mesh):
    placed = (
        P(None, "lat", "lon", None),
        P(None, "lat", "lon", None),
        P(None, "lat", "lon", None),
        P(None, None, "lat", "lon", None),
        P("lat", "lon", None),
        P("lat", "lon"),
    )
    return jax.shard_map(
        local, mesh=mesh, in_specs=placed, out_specs=P(None, "lat", "lon", None), check_vma=False
    )
```

```python
import functools

import jax
import jax.numpy as jnp
from jax import lax
from jax.experimental import pallas as pl
from jax.experimental.pallas import tpu as pltpu
from jax.sharding import PartitionSpec as P

HEAD_DIM = 128
REACH = 2
CAP = 4
MASKED = -1e30
FLOOR = -30000.0
SCALE2 = HEAD_DIM ** (-0.5) * 1.4426950408889634
FAR_LANE = 64
LOW_LANE = 12
EXP_LANE = 24
STAT = 128
CODE_ROWS = 16
ROUNDER = 12582912.0

VMEM = pl.BlockSpec(memory_space=pltpu.VMEM)
SMEM = pl.BlockSpec(memory_space=pltpu.SMEM)
ANY = pl.BlockSpec(memory_space=pl.ANY)
PARAMS = pltpu.CompilerParams(vmem_limit_bytes=48 * 1024 * 1024)


def call(body, out_shape, in_specs, *operands, scratch=()):
    single = not isinstance(out_shape, (list, tuple))
    return pl.pallas_call(
        body,
        out_shape=out_shape,
        in_specs=in_specs,
        out_specs=VMEM if single else [VMEM] * len(out_shape),
        scratch_shapes=list(scratch),
        compiler_params=PARAMS,
    )(*operands)


def columns(head):
    return pl.ds(head * HEAD_DIM, HEAD_DIM)


def dot_t(a, b):
    return lax.dot_general(a, b, (((1,), (1,)), ((), ())), preferred_element_type=jnp.float32)


def prep_queries(q_ref, ids_ref, out_ref, *, slots, sectors):
    rows = q_ref.shape[0] * q_ref.shape[1] * q_ref.shape[2]
    width = q_ref.shape[3]
    out_ref[:rows, :] = q_ref[...].reshape(rows, width)
    sector = lax.axis_index("lon")
    block = q_ref.shape[1] * q_ref.shape[2]
    lane_code = lax.broadcasted_iota(jnp.int32, (CODE_ROWS, width), 1) // block
    bias = jnp.full((CODE_ROWS, width), MASKED, jnp.float32)
    used = [jnp.int32(0), jnp.int32(0)]
    for e in range(ids_ref.shape[0]):
        entry = ids_ref[e]
        offset = lax.rem(entry // slots - sector + REACH + sectors, sectors)
        place = entry % slots
        for i, far_end in enumerate((0, 2 * REACH)):
            there = (offset == far_end) & (entry >= 0)
            place = jnp.where(offset == far_end, used[i], place)
            used[i] = used[i] + there.astype(jnp.int32)
        code = jnp.where(entry >= 0, offset * slots + place, -1)
        bias = jnp.where(lane_code == code, 0.0, bias)
    out_ref[rows:, :] = bias.astype(jnp.bfloat16)


def pack_blocks(bank_ref, first_ref, second_ref, outs, slots):
    rows = bank_ref.shape[0] // 2
    block = rows // slots
    sector = lax.axis_index("lon")
    straight = side_of(1) == side_of(REACH)
    for (mine_ref, cross_ref), out in zip(((first_ref, second_ref), (second_ref, first_ref)), outs):
        picks = [jnp.int32(0)] * CAP
        used = jnp.int32(0)
        for e in range(first_ref.shape[0]):
            entry = jnp.where(straight, mine_ref[e], cross_ref[e])
            named = (entry >= 0) & (entry // slots == sector)
            for p in range(CAP):
                picks[p] = jnp.where(named & (used == p), entry % slots, picks[p])
            used = used + named.astype(jnp.int32)
        for half in range(2):
            for p in range(CAP):
                start = pl.multiple_of(half * rows + picks[p] * block, block)
                out[pl.ds((half * CAP + p) * block, block), :] = bank_ref[pl.ds(start, block), :]


def prep_pair(k_ref, v_ref, _after, out_ref):
    rows = out_ref.shape[0] // 2
    out_ref[:rows, :] = k_ref[...].reshape(rows, out_ref.shape[1])
    out_ref[rows:, :] = v_ref[...].reshape(rows, out_ref.shape[1])


def prep_bank(bank_ref, out_ref):
    out_ref[...] = bank_ref[...].reshape(out_ref.shape)


def prep_packs(bank_ref, first_ref, second_ref, _one, _two, a_out, b_out, *, slots):
    pack_blocks(bank_ref, first_ref, second_ref, (a_out, b_out), slots)


def softmax_part(scores, values):
    largest = jnp.max(scores, axis=1, keepdims=True)
    weights = jnp.exp2((scores - largest) * SCALE2)
    total = jnp.sum(weights, axis=1, keepdims=True)
    mixed = jnp.dot(weights.astype(jnp.bfloat16), values, preferred_element_type=jnp.float32)
    return mixed, jnp.maximum(largest * SCALE2, FLOOR), total


def near_part(queries, tiles, head):
    band = lax.axis_index("lat")
    bands = lax.axis_size("lat")
    rows = tiles[0].shape[0] // 2
    meets = (band % 2 == 1) & (band < bands - 1) | (band % 2 == 0) & (band > 0)
    shut = jnp.where(meets, 0.0, MASKED).astype(jnp.float32)
    scores = [dot_t(queries, tile[:rows, columns(head)]) for tile in tiles]
    scores[2] = scores[2] + shut
    values = [tile[rows:, columns(head)] for tile in tiles]
    return softmax_part(jnp.concatenate(scores, axis=1), jnp.concatenate(values, axis=0))


def far_part(queries, ref, bias, head):
    rows = ref.shape[0] // 2
    scores = dot_t(queries, ref[:rows, columns(head)]) + bias
    return softmax_part(scores, ref[rows:, columns(head)])


def mask_of(q_ref, offset, keys, stride):
    rows = q_ref.shape[0] - CODE_ROWS
    return q_ref[rows:, pl.ds((offset + REACH) * stride, keys)].astype(jnp.float32)[:1]


def mask_for(q_ref, index, distance, keys, stride):
    down, up = (mask_of(q_ref, x, keys, stride) for x in (-distance, distance))
    above = (side_of() > 0) if index == 0 else (side_of() < 0)
    return jnp.where(above, down, up)


def lanes_of(rows):
    return lax.broadcasted_iota(jnp.int32, (rows, STAT), 1)


def peak_of(mixed):
    return jnp.max(jnp.abs(mixed), axis=1, keepdims=True)


def power_of(peak):
    return jnp.ceil(jnp.log2(jnp.maximum(peak, 1e-30)))


def put_code(out_ref, values, head):
    out_ref[:, columns(head)] = ((values + ROUNDER) - ROUNDER).astype(jnp.int32).astype(jnp.int16)


def coded_stats(level, power, heads):
    live = lanes_of(level.shape[0]) < heads
    whole = jnp.floor(level)
    low = jnp.minimum(jnp.floor((level - whole) * 32768.0), 32767.0)
    whole, low, power = (jnp.where(live, x, 0.0) for x in (whole, low, power))
    return whole + pltpu.roll(low, LOW_LANE, 1) + pltpu.roll(power, EXP_LANE, 1)


def put_stats(out_ref, stats):
    out_ref[:, out_ref.shape[1] - STAT :] = stats.astype(jnp.int32).astype(jnp.int16)


def near_sides(a_ref, b_ref, own_ref, mate_ref, other_ref, _after, a_out, b_out, a_mix, b_mix):
    rows = a_out.shape[0]
    heads = own_ref.shape[1] // HEAD_DIM
    lanes = lanes_of(rows)
    sides = ((a_out, a_mix), (b_out, b_mix))
    tops, totals, peaks = ([jnp.ones((rows, STAT), jnp.float32) for _ in sides] for _ in range(3))
    for head in range(heads):
        queries = jnp.concatenate([a_ref[:rows, columns(head)], b_ref[:rows, columns(head)]], axis=0)
        mixed, top, total = near_part(queries, (own_ref, mate_ref, other_ref), head)
        peak = peak_of(mixed)
        for i, (_, mix) in enumerate(sides):
            cut = slice(i * rows, (i + 1) * rows)
            mix[:, columns(head)] = mixed[cut]
            tops[i] = jnp.where(lanes == head, top[cut], tops[i])
            totals[i] = jnp.where(lanes == head, total[cut], totals[i])
            peaks[i] = jnp.where(lanes == head, peak[cut], peaks[i])
    for (out, mix), top, total, peak in zip(sides, tops, totals, peaks):
        inverse = 1.0 / total
        power = power_of(peak * inverse)
        scale = inverse * jnp.exp2(14.0 - power)
        put_stats(out, coded_stats(jnp.maximum(top + jnp.log2(total), FLOOR), power, heads))
        for head in range(heads):
            put_code(out, mix[:, columns(head)] * scale[:, head : head + 1], head)


def far_sides(a_ref, b_ref, bank_ref, _after, a_mix, b_mix, a_stat, b_stat):
    rows = a_mix.shape[0]
    keys = bank_ref.shape[0] // 2
    lanes = lanes_of(rows)
    for index, (ref, mix, stat) in enumerate(((a_ref, a_mix, a_stat), (b_ref, b_mix, b_stat))):
        bias = mask_for(ref, index, 1, keys, keys)
        packed = [jnp.zeros((rows, STAT), jnp.float32) for _ in range(3)]
        for head in range(bank_ref.shape[1] // HEAD_DIM):
            mixed, top, total = far_part(ref[:rows, columns(head)], bank_ref, bias, head)
            mix[:, columns(head)] = mixed
            packed = [
                jnp.where(lanes == head, x, p) for x, p in zip((top, total, peak_of(mixed)), packed)
            ]
        for i, p in enumerate(packed):
            stat[:, i * STAT : (i + 1) * STAT] = p


def far_beyond(
    a_ref, b_ref, a_part, b_part, a_stat, b_stat, a_pack, b_pack, _after, a_out, b_out, mix, *, keys
):
    rows, width = a_part.shape
    heads = width // HEAD_DIM
    packed = a_pack.shape[0] // 2
    masks = [mask_for(ref, index, 2, packed, keys) for index, ref in enumerate((a_ref, b_ref))]
    masks = [jnp.broadcast_to(mask, (rows, packed)) for mask in masks]
    closed = jnp.full((rows, packed), MASKED, jnp.float32)
    bias = jnp.concatenate(
        [jnp.concatenate([masks[0], closed], axis=1), jnp.concatenate([closed, masks[1]], axis=1)], axis=0
    )
    lanes = lanes_of(2 * rows)
    news = [jnp.zeros((2 * rows, STAT), jnp.float32) for _ in range(3)]
    for head in range(heads):
        cut = columns(head)
        queries = jnp.concatenate([a_ref[:rows, cut], b_ref[:rows, cut]], axis=0)
        far_keys = jnp.concatenate([b_pack[:packed, cut], a_pack[:packed, cut]], axis=0)
        far_values = jnp.concatenate([b_pack[packed:, cut], a_pack[packed:, cut]], axis=0)
        mixed, top, total = softmax_part(dot_t(queries, far_keys) + bias, far_values)
        mix[:, cut] = mixed
        news = [jnp.where(lanes == head, x, p) for x, p in zip((top, total, peak_of(mixed)), news)]
    lanes = lanes_of(rows)
    for index, (part, stat, out) in enumerate(((a_part, a_stat, a_out), (b_part, b_stat, b_out))):
        half = slice(index * rows, (index + 1) * rows)
        new = [x[half] for x in news]
        olds = [stat[:, i * STAT : (i + 1) * STAT] for i in range(3)]
        largest = jnp.maximum(olds[0], new[0])
        old_share, new_share = jnp.exp2(olds[0] - largest), jnp.exp2(new[0] - largest)
        total = jnp.where(lanes < heads, olds[1] * old_share + new[1] * new_share, 1.0)
        inverse = 1.0 / total
        old_share, new_share = old_share * inverse, new_share * inverse
        power = power_of(olds[2] * old_share + new[2] * new_share)
        scale = jnp.exp2(14.0 - power)
        old_share, new_share = old_share * scale, new_share * scale
        put_stats(out, coded_stats(jnp.maximum(largest + jnp.log2(total), FLOOR), power, heads))
        for head in range(heads):
            one, cut = slice(head, head + 1), columns(head)
            put_code(out, part[:, cut] * old_share[:, one] + mix[half, cut] * new_share[:, one], head)


def part_own(q_ref, own_ref, mate_ref, other_ref, bank_ref, _after, near_out, far_out, stat_out):
    rows = near_out.shape[0]
    keys = bank_ref.shape[0] // 2
    lanes = lanes_of(rows)
    bias = mask_of(q_ref, 0, keys, keys)
    tops = jnp.full((rows, STAT), FLOOR, jnp.float32)
    totals = jnp.ones((rows, STAT), jnp.float32)
    for head in range(own_ref.shape[1] // HEAD_DIM):
        queries = q_ref[:rows, columns(head)]
        for mixed, top, total, out, lane in (
            near_part(queries, (own_ref, mate_ref, other_ref), head) + (near_out, head),
            far_part(queries, bank_ref, bias, head) + (far_out, FAR_LANE + head),
        ):
            out[:, columns(head)] = mixed
            tops = jnp.where(lanes == lane, top, tops)
            totals = jnp.where(lanes == lane, total, totals)
    stat_out[:, :STAT] = jnp.maximum(tops + jnp.log2(totals), FLOOR)
    stat_out[:, STAT:] = 1.0 / totals


def shares_of(own_level, own_inverse, refs):
    levels, factors = [own_level], [own_inverse]
    for ref in refs:
        stat = ref[:, ref.shape[1] - STAT :].astype(jnp.int32).astype(jnp.float32)
        low = pltpu.roll(stat, STAT - LOW_LANE, 1)
        power = pltpu.roll(stat, STAT - EXP_LANE, 1)
        levels.append(stat + low * (1.0 / 32768.0))
        factors.append(jnp.exp2(power - 14.0))
    largest = functools.reduce(jnp.maximum, levels)
    weights = [jnp.exp2(level - largest) for level in levels]
    inverse = 1.0 / functools.reduce(jnp.add, weights)
    return [w * inverse * f for w, f in zip(weights, factors)]


def mixed_by(shares, own_ref, refs, head):
    one, cut = slice(head, head + 1), columns(head)
    total = own_ref[:, cut] * shares[0][:, one]
    for ref, share in zip(refs, shares[1:]):
        total += ref[:, cut].astype(jnp.int32).astype(jnp.float32) * share[:, one]
    return total


def merge_near(own_ref, stat_ref, a_ref, b_ref, out_ref):
    shares = shares_of(stat_ref[:, :STAT], stat_ref[:, STAT:], (a_ref, b_ref))
    for head in range(own_ref.shape[1] // HEAD_DIM):
        out_ref[:, columns(head)] = mixed_by(shares, own_ref, (a_ref, b_ref), head)


def merge_far(near_ref, own_ref, stat_ref, a_ref, b_ref, out_ref):
    own = [pltpu.roll(stat_ref[:, i * STAT : (i + 1) * STAT], STAT - FAR_LANE, 1) for i in range(2)]
    shares = shares_of(*own, (a_ref, b_ref))
    for head in range(own_ref.shape[1] // HEAD_DIM):
        total = near_ref[:, columns(head)] + mixed_by(shares, own_ref, (a_ref, b_ref), head)
        out_ref[:, :, :, columns(head)] = total.astype(jnp.bfloat16).reshape(out_ref.shape[:3] + (HEAD_DIM,))


def swapped(value, first, axis="lon", reach=1, closed=True):
    count = lax.axis_size(axis)
    pairs = []
    for i in range(count):
        up = (i // reach) % 2 == first
        partner = i + reach if up else i - reach
        if closed or 0 <= partner < count:
            pairs.append((i, partner % count))
    return lax.ppermute(value, axis, pairs)


def side_of(reach=1):
    return 1 - 2 * ((lax.axis_index("lon") // reach) % 2)


def local(queries, token_keys, token_values, memory_bank, memory_ids, memory_count):
    frames, band_rows, tile_cols, width = queries.shape
    rows = frames * band_rows * tile_cols
    slots = memory_bank.shape[1]
    sectors = lax.axis_size("lon")
    shape = jax.ShapeDtypeStruct

    entries = memory_ids.reshape(-1)
    wanted = jnp.where(jnp.arange(entries.shape[0]) < memory_count.reshape(()), entries, -1)
    block = band_rows * tile_cols
    keys = slots * block
    bank = call(prep_bank, shape((2 * keys, width), jnp.bfloat16), [VMEM], memory_bank)
    packs = shape((2 * CAP * block, width), jnp.bfloat16)
    queries_shape = shape((rows + CODE_ROWS, width), jnp.bfloat16)
    first, second = swapped(wanted, 0, reach=REACH), swapped(wanted, 1, reach=REACH)
    coded_queries = call(
        functools.partial(prep_queries, slots=slots, sectors=sectors), queries_shape, [VMEM, SMEM], queries, wanted
    )
    q_b, q_a = swapped(coded_queries, 1), swapped(coded_queries, 0)
    pack_a, pack_b = call(
        functools.partial(prep_packs, slots=slots), [packs, packs], [VMEM, SMEM, SMEM, ANY, ANY], bank, first, second, q_a, q_b
    )
    from_b, from_a = swapped(pack_b, 1), swapped(pack_a, 0)
    pair = call(
        prep_pair, shape((2 * rows, width), jnp.bfloat16), [VMEM, VMEM, ANY],
        token_keys, token_values, coded_queries,
    )
    other = swapped(pair, 1, "lat", closed=False)
    late = call(
        prep_pair, shape((2 * rows, width), jnp.bfloat16), [VMEM, VMEM, ANY],
        token_keys, token_values, first,
    )
    mate = swapped(late, 0, "lat", closed=False)
    plain = shape((rows, width), jnp.float32)
    work = pltpu.VMEM((rows, width), jnp.float32)
    coded = [shape((rows, width + STAT), jnp.int16)] * 2
    stats = shape((rows, 3 * STAT), jnp.float32)
    a_part, b_part, a_stat, b_stat = call(
        far_sides, [plain, plain, stats, stats], [VMEM] * 3 + [ANY], q_a, q_b, bank, coded_queries
    )
    a_near, b_near = call(
        near_sides, coded, [VMEM] * 5 + [ANY], q_a, q_b, pair, mate, other, a_stat, scratch=[work, work]
    )
    back_b_near, back_a_near = swapped(b_near, 1), swapped(a_near, 0)
    near, far, own_stat = call(
        part_own, [plain, plain, shape((rows, 2 * STAT), jnp.float32)], [VMEM] * 5 + [ANY],
        coded_queries, pair, mate, other, bank, a_near,
    )
    a_far, b_far = call(
        functools.partial(far_beyond, keys=keys), coded, [VMEM] * 8 + [ANY],
        q_a, q_b, a_part, b_part, a_stat, b_stat, from_a, from_b, own_stat,
        scratch=[pltpu.VMEM((2 * rows, width), jnp.float32)],
    )
    back_b_far, back_a_far = swapped(b_far, 1), swapped(a_far, 0)
    near = call(merge_near, plain, [VMEM] * 4, near, own_stat, back_a_near, back_b_near)
    return call(
        merge_far, shape(queries.shape, jnp.bfloat16), [VMEM] * 5, near, far, own_stat, back_a_far, back_b_far
    )


def solution(mesh):
    placed = (
        P(None, "lat", "lon", None),
        P(None, "lat", "lon", None),
        P(None, "lat", "lon", None),
        P(None, None, "lat", "lon", None),
        P("lat", "lon", None),
        P("lat", "lon"),
    )
    return jax.shard_map(
        local, mesh=mesh, in_specs=placed, out_specs=P(None, "lat", "lon", None), check_vma=False
    )
```

```python
import functools

import jax
import jax.numpy as jnp
from jax import lax
from jax.experimental import pallas as pl
from jax.experimental.pallas import tpu as pltpu
from jax.sharding import PartitionSpec as P

HEAD_DIM = 128
REACH = 2
CAP = 4
MASKED = -1e30
FLOOR = -30000.0
SCALE2 = HEAD_DIM ** (-0.5) * 1.4426950408889634
FAR_LANE = 64
LOW_LANE = 12
EXP_LANE = 24
STAT = 128
CODE_ROWS = 16
ROUNDER = 12582912.0

VMEM = pl.BlockSpec(memory_space=pltpu.VMEM)
SMEM = pl.BlockSpec(memory_space=pltpu.SMEM)
ANY = pl.BlockSpec(memory_space=pl.ANY)
PARAMS = pltpu.CompilerParams(vmem_limit_bytes=48 * 1024 * 1024)


def call(body, out_shape, in_specs, *operands, scratch=()):
    single = not isinstance(out_shape, (list, tuple))
    return pl.pallas_call(
        body,
        out_shape=out_shape,
        in_specs=in_specs,
        out_specs=VMEM if single else [VMEM] * len(out_shape),
        scratch_shapes=list(scratch),
        compiler_params=PARAMS,
    )(*operands)


def columns(head):
    return pl.ds(head * HEAD_DIM, HEAD_DIM)


def dot_t(a, b):
    return lax.dot_general(a, b, (((1,), (1,)), ((), ())), preferred_element_type=jnp.float32)


def prep_queries(q_ref, ids_ref, out_ref, *, slots, sectors):
    rows = q_ref.shape[0] * q_ref.shape[1] * q_ref.shape[2]
    width = q_ref.shape[3]
    out_ref[:rows, :] = q_ref[...].reshape(rows, width)
    sector = lax.axis_index("lon")
    block = q_ref.shape[1] * q_ref.shape[2]
    lane_code = lax.broadcasted_iota(jnp.int32, (CODE_ROWS, width), 1) // block
    bias = jnp.full((CODE_ROWS, width), MASKED, jnp.float32)
    used = [jnp.int32(0), jnp.int32(0)]
    for e in range(ids_ref.shape[0]):
        entry = ids_ref[e]
        offset = lax.rem(entry // slots - sector + REACH + sectors, sectors)
        place = entry % slots
        for i, far_end in enumerate((0, 2 * REACH)):
            there = (offset == far_end) & (entry >= 0)
            place = jnp.where(offset == far_end, used[i], place)
            used[i] = used[i] + there.astype(jnp.int32)
        code = jnp.where(entry >= 0, offset * slots + place, -1)
        bias = jnp.where(lane_code == code, 0.0, bias)
    out_ref[rows:, :] = bias.astype(jnp.bfloat16)


def pack_blocks(bank_ref, first_ref, second_ref, outs, slots):
    rows = bank_ref.shape[0] // 2
    block = rows // slots
    sector = lax.axis_index("lon")
    straight = side_of(1) == side_of(REACH)
    for (mine_ref, cross_ref), out in zip(((first_ref, second_ref), (second_ref, first_ref)), outs):
        picks = [jnp.int32(0)] * CAP
        used = jnp.int32(0)
        for e in range(first_ref.shape[0]):
            entry = jnp.where(straight, mine_ref[e], cross_ref[e])
            named = (entry >= 0) & (entry // slots == sector)
            for p in range(CAP):
                picks[p] = jnp.where(named & (used == p), entry % slots, picks[p])
            used = used + named.astype(jnp.int32)
        for half in range(2):
            for p in range(CAP):
                start = pl.multiple_of(half * rows + picks[p] * block, block)
                out[pl.ds((half * CAP + p) * block, block), :] = bank_ref[pl.ds(start, block), :]


def prep_pair(k_ref, v_ref, _after, out_ref):
    rows = out_ref.shape[0] // 2
    out_ref[:rows, :] = k_ref[...].reshape(rows, out_ref.shape[1])
    out_ref[rows:, :] = v_ref[...].reshape(rows, out_ref.shape[1])


def prep_bank(bank_ref, out_ref):
    out_ref[...] = bank_ref[...].reshape(out_ref.shape)


def prep_packs(bank_ref, first_ref, second_ref, _one, _two, a_out, b_out, *, slots):
    pack_blocks(bank_ref, first_ref, second_ref, (a_out, b_out), slots)


def softmax_part(scores, values):
    largest = jnp.max(scores, axis=1, keepdims=True)
    weights = jnp.exp2((scores - largest) * SCALE2)
    total = jnp.sum(weights, axis=1, keepdims=True)
    mixed = jnp.dot(weights.astype(jnp.bfloat16), values, preferred_element_type=jnp.float32)
    return mixed, jnp.maximum(largest * SCALE2, FLOOR), total


def near_part(queries, tiles, head):
    band = lax.axis_index("lat")
    bands = lax.axis_size("lat")
    rows = tiles[0].shape[0] // 2
    meets = (band % 2 == 1) & (band < bands - 1) | (band % 2 == 0) & (band > 0)
    shut = jnp.where(meets, 0.0, MASKED).astype(jnp.float32)
    scores = [dot_t(queries, tile[:rows, columns(head)]) for tile in tiles]
    scores[2] = scores[2] + shut
    values = [tile[rows:, columns(head)] for tile in tiles]
    return softmax_part(jnp.concatenate(scores, axis=1), jnp.concatenate(values, axis=0))


def far_part(queries, ref, bias, head):
    rows = ref.shape[0] // 2
    scores = dot_t(queries, ref[:rows, columns(head)]) + bias
    return softmax_part(scores, ref[rows:, columns(head)])


def mask_of(q_ref, offset, keys, stride):
    rows = q_ref.shape[0] - CODE_ROWS
    return q_ref[rows:, pl.ds((offset + REACH) * stride, keys)].astype(jnp.float32)[:1]


def mask_for(q_ref, index, distance, keys, stride):
    down, up = (mask_of(q_ref, x, keys, stride) for x in (-distance, distance))
    above = (side_of() > 0) if index == 0 else (side_of() < 0)
    return jnp.where(above, down, up)


def lanes_of(rows):
    return lax.broadcasted_iota(jnp.int32, (rows, STAT), 1)


def peak_of(mixed):
    return jnp.max(jnp.abs(mixed), axis=1, keepdims=True)


def power_of(peak):
    return jnp.ceil(jnp.log2(jnp.maximum(peak, 1e-30)))


def put_code(out_ref, values, head):
    out_ref[:, columns(head)] = ((values + ROUNDER) - ROUNDER).astype(jnp.int32).astype(jnp.int16)


def coded_stats(level, power, heads):
    live = lanes_of(level.shape[0]) < heads
    whole = jnp.floor(level)
    low = jnp.minimum(jnp.floor((level - whole) * 32768.0), 32767.0)
    whole, low, power = (jnp.where(live, x, 0.0) for x in (whole, low, power))
    return whole + pltpu.roll(low, LOW_LANE, 1) + pltpu.roll(power, EXP_LANE, 1)


def put_stats(out_ref, stats):
    out_ref[:, out_ref.shape[1] - STAT :] = stats.astype(jnp.int32).astype(jnp.int16)


def near_sides(a_ref, b_ref, own_ref, mate_ref, other_ref, _after, a_out, b_out, a_mix, b_mix):
    rows = a_out.shape[0]
    heads = own_ref.shape[1] // HEAD_DIM
    lanes = lanes_of(rows)
    sides = ((a_out, a_mix), (b_out, b_mix))
    tops, totals, peaks = ([jnp.ones((rows, STAT), jnp.float32) for _ in sides] for _ in range(3))
    for head in range(heads):
        queries = jnp.concatenate([a_ref[:rows, columns(head)], b_ref[:rows, columns(head)]], axis=0)
        mixed, top, total = near_part(queries, (own_ref, mate_ref, other_ref), head)
        peak = peak_of(mixed)
        for i, (_, mix) in enumerate(sides):
            cut = slice(i * rows, (i + 1) * rows)
            mix[:, columns(head)] = mixed[cut]
            tops[i] = jnp.where(lanes == head, top[cut], tops[i])
            totals[i] = jnp.where(lanes == head, total[cut], totals[i])
            peaks[i] = jnp.where(lanes == head, peak[cut], peaks[i])
    for (out, mix), top, total, peak in zip(sides, tops, totals, peaks):
        inverse = 1.0 / total
        power = power_of(peak * inverse)
        scale = inverse * jnp.exp2(14.0 - power)
        put_stats(out, coded_stats(jnp.maximum(top + jnp.log2(total), FLOOR), power, heads))
        for head in range(heads):
            put_code(out, mix[:, columns(head)] * scale[:, head : head + 1], head)


def far_sides(a_ref, b_ref, bank_ref, _after, a_mix, b_mix, a_stat, b_stat):
    rows = a_mix.shape[0]
    keys = bank_ref.shape[0] // 2
    lanes = lanes_of(rows)
    for index, (ref, mix, stat) in enumerate(((a_ref, a_mix, a_stat), (b_ref, b_mix, b_stat))):
        bias = mask_for(ref, index, 1, keys, keys)
        packed = [jnp.zeros((rows, STAT), jnp.float32) for _ in range(3)]
        for head in range(bank_ref.shape[1] // HEAD_DIM):
            mixed, top, total = far_part(ref[:rows, columns(head)], bank_ref, bias, head)
            mix[:, columns(head)] = mixed
            packed = [
                jnp.where(lanes == head, x, p) for x, p in zip((top, total, peak_of(mixed)), packed)
            ]
        for i, p in enumerate(packed):
            stat[:, i * STAT : (i + 1) * STAT] = p


def far_beyond(
    a_ref, b_ref, a_part, b_part, a_stat, b_stat, a_pack, b_pack, _after, a_out, b_out, mix, *, keys
):
    rows, width = a_part.shape
    heads = width // HEAD_DIM
    packed = a_pack.shape[0] // 2
    masks = [mask_for(ref, index, 2, packed, keys) for index, ref in enumerate((a_ref, b_ref))]
    masks = [jnp.broadcast_to(mask, (rows, packed)) for mask in masks]
    closed = jnp.full((rows, packed), MASKED, jnp.float32)
    bias = jnp.concatenate(
        [jnp.concatenate([masks[0], closed], axis=1), jnp.concatenate([closed, masks[1]], axis=1)], axis=0
    )
    lanes = lanes_of(2 * rows)
    news = [jnp.zeros((2 * rows, STAT), jnp.float32) for _ in range(3)]
    for head in range(heads):
        cut = columns(head)
        queries = jnp.concatenate([a_ref[:rows, cut], b_ref[:rows, cut]], axis=0)
        far_keys = jnp.concatenate([b_pack[:packed, cut], a_pack[:packed, cut]], axis=0)
        far_values = jnp.concatenate([b_pack[packed:, cut], a_pack[packed:, cut]], axis=0)
        mixed, top, total = softmax_part(dot_t(queries, far_keys) + bias, far_values)
        mix[:, cut] = mixed
        news = [jnp.where(lanes == head, x, p) for x, p in zip((top, total, peak_of(mixed)), news)]
    lanes = lanes_of(rows)
    for index, (part, stat, out) in enumerate(((a_part, a_stat, a_out), (b_part, b_stat, b_out))):
        half = slice(index * rows, (index + 1) * rows)
        new = [x[half] for x in news]
        olds = [stat[:, i * STAT : (i + 1) * STAT] for i in range(3)]
        largest = jnp.maximum(olds[0], new[0])
        old_share, new_share = jnp.exp2(olds[0] - largest), jnp.exp2(new[0] - largest)
        total = jnp.where(lanes < heads, olds[1] * old_share + new[1] * new_share, 1.0)
        inverse = 1.0 / total
        old_share, new_share = old_share * inverse, new_share * inverse
        power = power_of(olds[2] * old_share + new[2] * new_share)
        scale = jnp.exp2(14.0 - power)
        old_share, new_share = old_share * scale, new_share * scale
        put_stats(out, coded_stats(jnp.maximum(largest + jnp.log2(total), FLOOR), power, heads))
        for head in range(heads):
            one, cut = slice(head, head + 1), columns(head)
            put_code(out, part[:, cut] * old_share[:, one] + mix[half, cut] * new_share[:, one], head)


def part_own(q_ref, own_ref, mate_ref, other_ref, bank_ref, _after, near_out, far_out, stat_out):
    rows = near_out.shape[0]
    keys = bank_ref.shape[0] // 2
    lanes = lanes_of(rows)
    bias = mask_of(q_ref, 0, keys, keys)
    tops = jnp.full((rows, STAT), FLOOR, jnp.float32)
    totals = jnp.ones((rows, STAT), jnp.float32)
    for head in range(own_ref.shape[1] // HEAD_DIM):
        queries = q_ref[:rows, columns(head)]
        for mixed, top, total, out, lane in (
            near_part(queries, (own_ref, mate_ref, other_ref), head) + (near_out, head),
            far_part(queries, bank_ref, bias, head) + (far_out, FAR_LANE + head),
        ):
            out[:, columns(head)] = mixed
            tops = jnp.where(lanes == lane, top, tops)
            totals = jnp.where(lanes == lane, total, totals)
    stat_out[:, :STAT] = jnp.maximum(tops + jnp.log2(totals), FLOOR)
    stat_out[:, STAT:] = 1.0 / totals


def shares_of(own_level, own_inverse, refs):
    levels, factors = [own_level], [own_inverse]
    for ref in refs:
        stat = ref[:, ref.shape[1] - STAT :].astype(jnp.int32).astype(jnp.float32)
        low = pltpu.roll(stat, STAT - LOW_LANE, 1)
        power = pltpu.roll(stat, STAT - EXP_LANE, 1)
        levels.append(stat + low * (1.0 / 32768.0))
        factors.append(jnp.exp2(power - 14.0))
    largest = functools.reduce(jnp.maximum, levels)
    weights = [jnp.exp2(level - largest) for level in levels]
    inverse = 1.0 / functools.reduce(jnp.add, weights)
    return [w * inverse * f for w, f in zip(weights, factors)]


def mixed_by(shares, own_ref, refs, head):
    one, cut = slice(head, head + 1), columns(head)
    total = own_ref[:, cut] * shares[0][:, one]
    for ref, share in zip(refs, shares[1:]):
        total += ref[:, cut].astype(jnp.int32).astype(jnp.float32) * share[:, one]
    return total


def merge_near(own_ref, stat_ref, b_ref, a_ref, out_ref):
    shares = shares_of(stat_ref[:, :STAT], stat_ref[:, STAT:], (a_ref, b_ref))
    for head in range(own_ref.shape[1] // HEAD_DIM):
        out_ref[:, columns(head)] = mixed_by(shares, own_ref, (a_ref, b_ref), head)


def merge_far(near_ref, own_ref, stat_ref, a_ref, b_ref, out_ref):
    own = [pltpu.roll(stat_ref[:, i * STAT : (i + 1) * STAT], STAT - FAR_LANE, 1) for i in range(2)]
    shares = shares_of(*own, (a_ref, b_ref))
    for head in range(own_ref.shape[1] // HEAD_DIM):
        total = near_ref[:, columns(head)] + mixed_by(shares, own_ref, (a_ref, b_ref), head)
        out_ref[:, :, :, columns(head)] = total.astype(jnp.bfloat16).reshape(out_ref.shape[:3] + (HEAD_DIM,))


def swapped(value, first, axis="lon", reach=1, closed=True):
    count = lax.axis_size(axis)
    pairs = []
    for i in range(count):
        up = (i // reach) % 2 == first
        partner = i + reach if up else i - reach
        if closed or 0 <= partner < count:
            pairs.append((i, partner % count))
    return lax.ppermute(value, axis, pairs)


def side_of(reach=1):
    return 1 - 2 * ((lax.axis_index("lon") // reach) % 2)


def local(queries, token_keys, token_values, memory_bank, memory_ids, memory_count):
    frames, band_rows, tile_cols, width = queries.shape
    rows = frames * band_rows * tile_cols
    slots = memory_bank.shape[1]
    sectors = lax.axis_size("lon")
    shape = jax.ShapeDtypeStruct

    entries = memory_ids.reshape(-1)
    wanted = jnp.where(jnp.arange(entries.shape[0]) < memory_count.reshape(()), entries, -1)
    block = band_rows * tile_cols
    keys = slots * block
    bank = call(prep_bank, shape((2 * keys, width), jnp.bfloat16), [VMEM], memory_bank)
    packs = shape((2 * CAP * block, width), jnp.bfloat16)
    queries_shape = shape((rows + CODE_ROWS, width), jnp.bfloat16)
    first, second = swapped(wanted, 0, reach=REACH), swapped(wanted, 1, reach=REACH)
    coded_queries = call(
        functools.partial(prep_queries, slots=slots, sectors=sectors), queries_shape, [VMEM, SMEM], queries, wanted
    )
    q_b, q_a = swapped(coded_queries, 1), swapped(coded_queries, 0)
    pack_a, pack_b = call(
        functools.partial(prep_packs, slots=slots), [packs, packs], [VMEM, SMEM, SMEM, ANY, ANY], bank, first, second, q_a, q_b
    )
    from_b, from_a = swapped(pack_b, 1), swapped(pack_a, 0)
    pair = call(
        prep_pair, shape((2 * rows, width), jnp.bfloat16), [VMEM, VMEM, ANY],
        token_keys, token_values, coded_queries,
    )
    other = swapped(pair, 1, "lat", closed=False)
    late = call(
        prep_pair, shape((2 * rows, width), jnp.bfloat16), [VMEM, VMEM, ANY],
        token_keys, token_values, first,
    )
    mate = swapped(late, 0, "lat", closed=False)
    plain = shape((rows, width), jnp.float32)
    work = pltpu.VMEM((rows, width), jnp.float32)
    coded = [shape((rows, width + STAT), jnp.int16)] * 2
    stats = shape((rows, 3 * STAT), jnp.float32)
    a_part, b_part, a_stat, b_stat = call(
        far_sides, [plain, plain, stats, stats], [VMEM] * 3 + [ANY], q_a, q_b, bank, coded_queries
    )
    a_near, b_near = call(
        near_sides, coded, [VMEM] * 5 + [ANY], q_a, q_b, pair, mate, other, a_stat, scratch=[work, work]
    )
    back_b_near, back_a_near = swapped(b_near, 1), swapped(a_near, 0)
    near, far, own_stat = call(
        part_own, [plain, plain, shape((rows, 2 * STAT), jnp.float32)], [VMEM] * 5 + [ANY],
        coded_queries, pair, mate, other, bank, a_near,
    )
    a_far, b_far = call(
        functools.partial(far_beyond, keys=keys), coded, [VMEM] * 8 + [ANY],
        q_a, q_b, a_part, b_part, a_stat, b_stat, from_a, from_b, own_stat,
        scratch=[pltpu.VMEM((2 * rows, width), jnp.float32)],
    )
    back_b_far, back_a_far = swapped(b_far, 1), swapped(a_far, 0)
    near = call(merge_near, plain, [VMEM] * 4, near, own_stat, back_b_near, back_a_near)
    return call(
        merge_far, shape(queries.shape, jnp.bfloat16), [VMEM] * 5, near, far, own_stat, back_a_far, back_b_far
    )


def solution(mesh):
    placed = (
        P(None, "lat", "lon", None),
        P(None, "lat", "lon", None),
        P(None, "lat", "lon", None),
        P(None, None, "lat", "lon", None),
        P("lat", "lon", None),
        P("lat", "lon"),
    )
    return jax.shard_map(
        local, mesh=mesh, in_specs=placed, out_specs=P(None, "lat", "lon", None), check_vma=False
    )
```
